1024 devices in a mesh: dp: 8 (over y, core), ctx: 4 (over x), expert: 32 (over z).
Axes of the slice: x: 4, y: 4, z: 32, core: 2. Of those that a mesh axis runs over, the one named last changes fastest.
Arguments:
- out_grad: bfloat16 [8192, 7168], P(('ctx', 'expert'), 'dp'), may hold values from -6 to 6
- expert_ids: int32 [8192, 8], P(('ctx', 'expert')), may hold values from 0 to 31, all different within a row; in each aligned block of 64 rows (0 to 63, 64 to 127, ...) at most 32 rows name the same one
- gates: bfloat16 [8192, 8], P(('ctx', 'expert')), may hold values from 0.049804688 to 1
- hidden_saved: bfloat16 [131072, 1024], P(('ctx', 'expert')), may hold values from -0.1796875 to 0.1796875
- w_down: bfloat16 [32, 1024, 7168], P('expert', None, 'dp'), may hold values from -0.0625 to 0.0625
Outputs:
- d_hidden: bfloat16 [131072, 1024], P(('ctx', 'expert'), 'dp')
- w_grad: float32 [32, 1024, 7168], P('expert', 'ctx', 'dp')
- gate_grad: float32 [8192, 8], P(('ctx', 'expert'))
The draws below stay inside these ranges and needn't reach their ends.
Inputs may be any that keep to these rules, and one draw needn't show every extreme that they name: `expert_ids`: each token names 8 different experts. Among the 64 x 8 choices of one device's tokens, no expert is named more than 32 times, a bound that some block reaches.
All inputs are finite; a program needn't handle non-finite values.
Results may differ from the reference program's by a relative error of at most 0.019.
Values may be sent and summed in bfloat16 or wider, within the bound.
A program may use at most 32 MiB of HBM per device.

```python
import math
import jax
import jax.numpy as jnp
import numpy as np
from jax import lax

D = 7168
FF = 1024
TOP = 8
TOK_DEV = 64
EXPERTS = 32
CAP = 32
SLOTS = 1024
TOKENS = 8192
ROWS = 131072
BLOCK_D = 896
N_DP = 8
N_CTX = 4
N_EXPERT = 32


def block_levels(rng, extent, shards, least, high):
    factor_of, own = 1.0, jax.random.fold_in(rng, 6)
    for position, parts in shards:
        steps = jnp.exp(jax.random.uniform(jax.random.fold_in(own, position), (parts,), jnp.float32, least / len(shards), high / len(shards)))
        factor_of = factor_of * jnp.repeat(steps, extent[position] // parts).reshape([-1 if axis == position else 1 for axis in range(len(extent))])
    return factor_of


def assign_block(key, own, number, rows, count, top, limit, lean):
    order = jax.random.permutation(key, count)
    crowded, ordinary = shares(count, rows * top, limit, lean, True), shares(count, rows * top, limit, lean, False)
    places = jnp.arange(count)

    def named(lengths, rotation):
        used = int((lengths > 0).sum())
        fixed = max(1, used // 4)
        moved = fixed + (places - fixed + rotation * (used - fixed)) % max(1, count - fixed)
        return jnp.zeros((count,), jnp.int32).at[order[jnp.where(places < fixed, places, moved)]].set(jnp.asarray(lengths, jnp.int32))

    lengths = jnp.where(number % 4 == 0, named(crowded, number // 4), named(ordinary, number - number // 4 - 1))
    mixed = jax.random.permutation(jax.random.fold_in(own, 3), count)
    donor, sink = mixed[0:count // 2 * 2:2], mixed[1:count // 2 * 2:2]
    room = jnp.minimum(lengths[donor] - 1, limit - lengths[sink]) // 2
    room = jnp.where((donor == order[0]) | (sink == order[0]) | (lengths[sink] == 0), 0, jnp.maximum(room, 0))
    moved = jax.random.randint(jax.random.fold_in(own, 4), (count // 2,), 0, 1 << 20) % (room + 1)
    lengths = lengths.at[donor].add(-moved).at[sink].add(moved)
    items = jnp.searchsorted(jnp.cumsum(lengths), jnp.arange(rows * top), side="right").astype(jnp.int32)
    listing = items.reshape(top, rows).T
    listing = listing[jax.random.permutation(jax.random.fold_in(own, 1), rows)]
    rotation = jax.random.randint(jax.random.fold_in(own, 2), (rows, 1), 0, top)
    return jnp.take_along_axis(listing, (jnp.arange(top)[None, :] + rotation) % top, axis=1)


def shares(count, total, most, slope, full):
    weights = [(1 << 20) // math.isqrt(standing ** slope) + 1 for standing in range(1, count + 1)]
    largest = most if full else min(most, max(-(-total // count), total * weights[0] // sum(weights)))
    least = 1 if total - largest >= count - 1 else 0
    counts, spare = [largest] + [least] * (count - 1), total - largest - least * (count - 1)
    while spare > 0:
        free = [i for i in range(1, count) if counts[i] < largest] or [i for i in range(1, count) if counts[i] < most]
        pool, budget = sum([weights[i] for i in free]), spare
        for i in free:
            more = min(most - counts[i], max(1, budget * weights[i] // pool), spare)
            counts[i] = counts[i] + more
            spare = spare - more
    return np.array(counts)


def scatter_about(key, dims, deviation, bound, shards=(), kind=jnp.bfloat16):
    entries = deviation * jax.random.normal(key, dims, jnp.float32)
    if shards:
        entries = entries * block_levels(key, dims, shards, -0.22, 0.18)
    return jnp.clip(entries, -bound, bound).astype(kind)


def setup_inputs(seed: int = 0) -> dict:
    keys = jax.random.split(jax.random.key(seed), 6)
    out_grad = scatter_about(keys[0], (TOKENS, D), 1.0, 6.0, ((0, 128), (1, 8)))
    expert_ids_keys = jax.random.split(jax.random.fold_in(keys[1], 1), TOKENS // TOK_DEV)
    expert_ids_turns = jax.random.permutation(jax.random.fold_in(keys[1], 3), TOKENS // TOK_DEV)
    expert_ids = jax.vmap(lambda own, number: assign_block(jax.random.fold_in(keys[1], 2), own, number, TOK_DEV, EXPERTS, TOP, CAP, 2))(expert_ids_keys, expert_ids_turns).reshape((TOKENS, TOP))
    gates = jnp.clip(jnp.exp(math.log(1.0) - 2.9996462 * jax.random.uniform(keys[2], (TOKENS, TOP), jnp.float32) ** block_levels(keys[2], (TOKENS, TOP), ((0, 128),), -0.2, 0.2)), 0.049804688, 1.0).astype(jnp.bfloat16)
    hidden_saved = scatter_about(keys[3], (ROWS, FF), 0.03, 0.1796875, ((0, 128),))
    w_down = scatter_about(keys[4], (EXPERTS, FF, D), D ** -0.5, 0.0625, ((0, 32), (2, 8)))
    return dict(out_grad=out_grad, expert_ids=expert_ids, gates=gates, hidden_saved=hidden_saved, w_down=w_down)


def row_targets(expert_ids):
    block_count = N_CTX * N_EXPERT
    choice_ids = expert_ids.reshape(block_count, TOK_DEV * TOP).astype(jnp.int32)
    onehot = (choice_ids[:, :, None] == jnp.arange(EXPERTS, dtype=jnp.int32)[None, None, :]).astype(jnp.int32)
    earlier = jnp.cumsum(onehot, axis=1) - onehot
    slot_index = jnp.sum(earlier * onehot, axis=2).astype(jnp.int32)
    block_index = jnp.arange(block_count, dtype=jnp.int32)
    group_index = (block_index // N_EXPERT)[:, None]
    source = (block_index % N_EXPERT)[:, None]
    target = ((group_index * EXPERTS + choice_ids) * N_EXPERT + source) * CAP + slot_index
    return target.reshape(-1).astype(jnp.int32)


def by_expert(values):
    rest = values.shape[1:]
    shaped = values.reshape((N_CTX, EXPERTS, SLOTS) + rest)
    moved = jnp.moveaxis(shaped, 1, 0)
    return moved.reshape((EXPERTS, N_CTX * SLOTS) + rest)


def from_expert(values):
    rest = values.shape[2:]
    shaped = values.reshape((EXPERTS, N_CTX, SLOTS) + rest)
    moved = jnp.moveaxis(shaped, 0, 1)
    return moved.reshape((ROWS,) + rest)


def reference(out_grad, expert_ids, gates, hidden_saved, w_down):
    target = row_targets(expert_ids)
    choice_count = TOKENS * TOP
    owner_index = jnp.full((ROWS,), choice_count, jnp.int32).at[target].set(jnp.arange(choice_count, dtype=jnp.int32))
    alive = owner_index < choice_count
    clipped = jnp.minimum(owner_index, choice_count - 1)
    token_index = (clipped // TOP).astype(jnp.int32)
    gate_flat = gates.reshape(-1).astype(jnp.float32)
    gate_rows = jnp.where(alive, gate_flat[clipped], jnp.float32(0.0))
    inputs = (by_expert(token_index), by_expert(alive), by_expert(gate_rows), by_expert(hidden_saved), w_down)

    def one_expert(pieces):
        tok_rows, live_rows, gate_here, hidden, weight = pieces
        routed = jnp.where(live_rows[:, None], out_grad[tok_rows], jnp.zeros((), jnp.bfloat16))
        routed_wide = routed.astype(jnp.float32)
        weight_wide = weight.astype(jnp.float32)
        running = jnp.zeros((routed.shape[0], FF), jnp.float32)
        for block_index in range(N_DP):
            lower = block_index * BLOCK_D
            upper = lower + BLOCK_D
            partial_value = jnp.dot(routed_wide[:, lower:upper], weight_wide[:, lower:upper].T, precision=lax.Precision.HIGHEST)
            rounded = lax.optimization_barrier(partial_value.astype(jnp.bfloat16))
            running = running + rounded.astype(jnp.float32)
        hidden_grad = (gate_here[:, None] * running).astype(jnp.bfloat16)
        hidden_wide = hidden.astype(jnp.float32)
        row_gate = jnp.sum(hidden_wide * running, axis=1)
        scaled = (gate_here[:, None] * routed_wide).astype(jnp.bfloat16).astype(jnp.float32)
        weight_grad = jnp.zeros((FF, D), jnp.float32)
        for group_index in range(N_CTX):
            lower = group_index * SLOTS
            upper = lower + SLOTS
            contribution = jnp.dot(hidden_wide[lower:upper].T, scaled[lower:upper], precision=lax.Precision.HIGHEST)
            rounded = lax.optimization_barrier(contribution.astype(jnp.bfloat16))
            weight_grad = weight_grad + rounded.astype(jnp.float32)
        return hidden_grad, row_gate, weight_grad

    hidden_grads, row_gates, w_grad = lax.map(one_expert, inputs)
    d_hidden = from_expert(hidden_grads)
    gate_grad = from_expert(row_gates)[target].reshape(TOKENS, TOP)
    return d_hidden, w_grad, gate_grad
```

```python
import functools

import jax
import jax.numpy as jnp
from jax import lax
from jax.experimental import pallas as pl
from jax.experimental.pallas import tpu as pltpu
from jax.sharding import PartitionSpec as P

MESH = pl.DeviceIdType.MESH
BF = jnp.bfloat16
F32 = jnp.float32

NZ = 32
NC = 4
ND = 8
TOK = 64
CAP = 32
FF = 1024
WID = 896
TILES = WID // 128
SH = FF // ND
FQ = FF // NC
META = 16
ROWS = META + TOK * TILES
GB = 8
NG = NZ // GB
GR = GB * CAP
GT = GB * TOK
CHUNKS = ((0, META + 2 * TOK), (META + 2 * TOK, 2 * TOK), (META + 4 * TOK, 2 * TOK), (META + 6 * TOK, TOK))
NCH = len(CHUNKS)


def kernel(
    x_ref, ids_ref, gates_ref, hid_hbm, w_hbm,
    dh_ref, wg_ref, gg_ref,
    gat, hid, wv, acc, rows_s, scaled_s, pown, sel_s, gcol_s,
    pbuf, prec, qbuf, qrec, gsend, gback, part_s, parts,
    xa, xb1, xb2, ra, rb1, rb2,
    load_sem, zs, zr, cs, cr, ys, yr, gs, gr, ps, pr, xs, xr,
):
    z = lax.axis_index("expert")
    dp = lax.axis_index("dp")
    cx = lax.axis_index("ctx")
    core = lax.rem(dp, 2)
    yy = dp // 2
    zright = lax.rem(z + 1, NZ)
    zleft = lax.rem(z + NZ - 1, NZ)
    cright = lax.rem(cx + 1, NC)
    cleft = lax.rem(cx + NC - 1, NC)
    copp = lax.rem(cx + 2, NC)
    partner = dp + 1 - 2 * core

    barrier = pltpu.get_barrier_semaphore()
    for nb in (zright, zleft):
        pl.semaphore_signal(barrier, inc=1, device_id={"expert": nb}, device_id_type=MESH)
    for nb in (cright, cleft):
        pl.semaphore_signal(barrier, inc=1, device_id={"ctx": nb}, device_id_type=MESH)
    for i in range(1, ND):
        pl.semaphore_signal(
            barrier, inc=1, device_id={"dp": lax.rem(dp + i, ND)}, device_id_type=MESH
        )

    loads = (
        pltpu.make_async_copy(hid_hbm, hid, load_sem.at[0]),
        pltpu.make_async_copy(w_hbm.at[:, core], wv.at[0], load_sem.at[1]),
        pltpu.make_async_copy(w_hbm.at[:, 1 - core], wv.at[1], load_sem.at[2]),
    )
    for load in loads:
        load.start()

    e_iota = lax.broadcasted_iota(jnp.int32, (NZ, TOK), 0)
    gate_tab = jnp.zeros((NZ, TOK), F32)
    gates = gates_ref[...].astype(F32)
    for k in range(8):
        gate_tab = gate_tab + jnp.where(e_iota == ids_ref[k : k + 1, :], gates[k : k + 1, :], 0.0)
    gat[0, 0:META, :] = jnp.concatenate([gate_tab[0:META], gate_tab[META:]], axis=1).astype(BF)
    for j in range(TILES):
        gat[0, META + j * TOK : META + (j + 1) * TOK, :] = x_ref[:, j * 128 : (j + 1) * 128]

    pl.semaphore_wait(barrier, 4 + ND - 1)

    def hop(d, c, k):
        lo, n = CHUNKS[c]
        if d == 0:
            src, dst, dev = jnp.maximum(2 * k - 1, 0), 2 * k + 1, zright
        else:
            src, dst, dev = 2 * k, 2 * k + 2, zleft
        return pltpu.make_async_remote_copy(
            src_ref=gat.at[src, pl.ds(lo, n)],
            dst_ref=gat.at[dst, pl.ds(lo, n)],
            send_sem=zs.at[d, c, k],
            recv_sem=zr.at[d, c, k],
            device_id={"expert": dev},
            device_id_type=MESH,
        )

    for c in range(NCH):
        for d in range(2):
            hop(d, c, jnp.int32(0)).start()

    for load in loads:
        load.wait()
    acc[...] = jnp.zeros_like(acc)

    def ring_step(k):
        for c in range(NCH):
            hop(0, c, k).wait_recv()

            @pl.when(k < 15)
            def _():
                hop(0, c, k + 1).start()
                hop(1, c, k).wait_recv()

            @pl.when(k < 14)
            def _():
                hop(1, c, k + 1).start()

    def source_of(g, i):
        dist = GB // 2 * g + (i + 1) // 2
        return lax.rem(z + dist if i % 2 == 0 else z - dist + NZ, NZ)

    def rows_of_group(g):
        base = g * GB
        lane = lax.broadcasted_iota(jnp.int32, (GB, 128), 1)
        row = lax.broadcasted_iota(jnp.int32, (GB, 128), 0)
        tab = gat[pl.ds(base, GB), 0:META, :].astype(F32)
        sub = lax.broadcasted_iota(jnp.int32, (GB, META, 128), 1)
        mine = jnp.sum(jnp.where(sub == lax.rem(z, META), tab, 0.0), axis=1)
        odd = lax.rem(row, 2)
        mine = jnp.where(odd == z // META, mine, pltpu.roll(mine, TOK, 1))
        mine = jnp.where(lane // TOK == odd, mine, 0.0)
        named = mine > 0.0
        t0 = lax.broadcasted_iota(jnp.int32, (128, 128), 0)
        t1 = lax.broadcasted_iota(jnp.int32, (128, 128), 1)
        before = jnp.where((t0 < t1) & (t0 // TOK == t1 // TOK), 1.0, 0.0).astype(BF)
        count = jnp.dot(
            jnp.where(named, 1.0, 0.0).astype(BF), before, preferred_element_type=F32
        ).astype(jnp.int32)
        target = jnp.where(named, lax.rem(row, 4) * CAP + count, -1)
        slot = lax.broadcasted_iota(jnp.int32, (128, 128), 0)
        for h in range(2):
            sel, gsel = [], []
            for j in range(2):
                a = 4 * h + 2 * j
                t = jnp.maximum(target[a : a + 1], target[a + 1 : a + 2])
                gv = mine[a : a + 1] + mine[a + 1 : a + 2]
                one = slot == t
                sel.append(jnp.where(one, 1.0, 0.0))
                gsel.append(jnp.where(one, gv, 0.0))
            sel = jnp.concatenate(sel, axis=1)
            gsel = jnp.concatenate(gsel, axis=1)
            sel_s[h] = sel
            gcol_s[h * 128 : (h + 1) * 128, :] = jnp.sum(gsel, axis=1, keepdims=True)
            sel = sel.astype(BF)
            gsel = gsel.astype(BF)
            for j in range(TILES):
                xt = gat[
                    pl.ds(base + 4 * h, 4), META + j * TOK : META + (j + 1) * TOK, :
                ].reshape(4 * TOK, 128)
                cols = slice(j * 128, (j + 1) * 128)
                rows_s[h * 128 : (h + 1) * 128, cols] = jnp.dot(
                    sel, xt, preferred_element_type=F32
                ).astype(BF)
                scaled_s[h * 128 : (h + 1) * 128, cols] = jnp.dot(
                    gsel, xt, preferred_element_type=F32
                ).astype(BF)

    def partial_of(which, y):
        return lax.dot_general(
            rows_s[...], wv[which, y], (((1,), (1,)), ((), ())), preferred_element_type=F32
        )

    def to_partner(g):
        return pltpu.make_async_remote_copy(
            src_ref=pbuf.at[g],
            dst_ref=prec.at[g],
            send_sem=cs.at[g],
            recv_sem=cr.at[g],
            device_id={"dp": partner},
            device_id_type=MESH,
        )

    def to_y(g, i):
        return pltpu.make_async_remote_copy(
            src_ref=qbuf.at[g, i - 1],
            dst_ref=qrec.at[g, i - 1],
            send_sem=ys.at[g, i - 1],
            recv_sem=yr.at[g, i - 1],
            device_id={"dp": lax.rem(dp + 2 * i, ND)},
            device_id_type=MESH,
        )

    def send_partials(g):
        for y in range(4):
            pbuf[g, y] = partial_of(1, y).astype(BF)
        to_partner(g).start()

    def own_partials():
        for y in range(4):
            pown[y] = partial_of(0, y).astype(BF)

    def contribute(g, share):
        parts_h = [
            hid[source_of(g, i), :, pl.ds(pl.multiple_of(share * FQ, FQ), FQ)] for i in range(GB)
        ]
        acc[share] += lax.dot_general(
            jnp.concatenate(parts_h, axis=0),
            scaled_s[...],
            (((0,), (0,)), ((), ())),
            preferred_element_type=F32,
        )

    def sum_cores(g):
        to_partner(g).wait_recv()
        for i in range(1, 4):
            y = lax.rem(yy + i, 4)
            qbuf[g, i - 1] = (pown[y].astype(F32) + prec[g, y].astype(F32)).astype(BF)
            to_y(g, i).start()

    def to_home(p, s):
        return pltpu.make_async_remote_copy(
            src_ref=gsend.at[p // 2],
            dst_ref=gback.at[z],
            send_sem=gs.at[p],
            recv_sem=gr.at[z],
            device_id={"expert": s},
            device_id_type=MESH,
        )

    def finish_rows(g):
        total = pown[yy].astype(F32) + prec[g, yy].astype(F32)
        for i in range(1, 4):
            to_y(g, i).wait_recv()
            total = total + qrec[g, i - 1].astype(F32)
        dh = (gcol_s[...] * total).astype(BF)
        own = []
        for i in range(GB):
            s = source_of(g, i)
            dh_ref[s] = dh[i * CAP : (i + 1) * CAP]
            own.append(hid[s, :, pl.ds(pl.multiple_of(dp * SH, SH), SH)])
        own = jnp.concatenate(own, axis=0).astype(F32)
        col = jnp.sum(own * total, axis=1, keepdims=True)
        for h in range(2):
            back = jnp.sum(sel_s[h] * col[h * 128 : (h + 1) * 128], axis=0, keepdims=True)
            for j in range(2):
                gsend[g * 4 + 2 * h + j] = back[:, j * 128 : (j + 1) * 128]
        for i in range(GB):
            p = g * GB + i
            if i == 0:

                @pl.when(g > 0)
                def _():
                    to_home(p, source_of(g, i)).start()

                @pl.when(g == 0)
                def _():
                    gback[z] = gsend[0]
            else:
                to_home(p, source_of(g, i)).start()

    @pl.loop(0, NG)
    def _(g):
        ring_step(4 * g)

        @pl.when(g > 0)
        def _():
            rows_of_group(g - 1)
            send_partials(g - 1)

        ring_step(4 * g + 1)

        @pl.when(g > 0)
        def _():
            own_partials()
            contribute(g - 1, jnp.int32(0))
            contribute(g - 1, jnp.int32(1))

        ring_step(4 * g + 2)

        @pl.when(g > 0)
        def _():
            contribute(g - 1, jnp.int32(2))
            contribute(g - 1, jnp.int32(3))
            sum_cores(g - 1)

        ring_step(4 * g + 3)

        @pl.when(g > 0)
        def _():
            finish_rows(g - 1)

    half = FQ // 2

    def to_x(kind, d):
        src = (xa, xb1, xb2)[kind]
        dst = (ra, rb1, rb2)[kind]
        return pltpu.make_async_remote_copy(
            src_ref=src.at[d],
            dst_ref=dst.at[d],
            send_sem=xs.at[kind, d],
            recv_sem=xr.at[kind, d],
            device_id={"ctx": (cright, cleft)[d]},
            device_id_type=MESH,
        )

    last = jnp.int32(NG - 1)
    rows_of_group(last)
    contribute(last, copp)
    for d in range(2):
        xa[d] = acc[copp, d * half : (d + 1) * half].astype(BF)
        to_x(0, d).start()
    send_partials(last)
    contribute(last, cright)
    contribute(last, cleft)
    xb1[0] = acc[cright, half:].astype(BF)
    to_x(1, 0).start()
    xb1[1] = acc[cleft, :half].astype(BF)
    to_x(1, 1).start()
    own_partials()
    sum_cores(last)
    to_x(0, 0).wait_recv()
    xb2[0] = (acc[cright, :half] + ra[0].astype(F32)).astype(BF)
    to_x(2, 0).start()
    to_x(0, 1).wait_recv()
    xb2[1] = (acc[cleft, half:] + ra[1].astype(F32)).astype(BF)
    to_x(2, 1).start()
    contribute(last, cx)
    finish_rows(last)

    def from_home(e):
        return pltpu.make_async_remote_copy(
            src_ref=gsend.at[0],
            dst_ref=gback.at[e],
            send_sem=gs.at[0],
            recv_sem=gr.at[e],
            device_id={"expert": e},
            device_id_type=MESH,
        )

    @pl.loop(1, NZ)
    def _(i):
        from_home(lax.rem(z + i, NZ)).wait_recv()

    back = gback[...].reshape(NZ, 128)
    e2 = lax.broadcasted_iota(jnp.int32, (NZ, 128), 0)
    dist = lax.rem(e2 - z + NZ, NZ)
    swap = (dist >= 1) & (dist <= NZ // 2)
    back = jnp.where(swap, pltpu.roll(back, TOK, 1), back)[:, 0:TOK]
    mine = []
    for k in range(8):
        mine.append(
            jnp.sum(jnp.where(e_iota == ids_ref[k : k + 1, :], back, 0.0), axis=0, keepdims=True)
        )
    mine = jnp.concatenate(mine, axis=0)
    part_s[...] = jnp.concatenate([mine, jnp.zeros_like(mine)], axis=1)

    def to_dp(i):
        return pltpu.make_async_remote_copy(
            src_ref=part_s,
            dst_ref=parts.at[i - 1],
            send_sem=ps.at[i - 1],
            recv_sem=pr.at[i - 1],
            device_id={"dp": lax.rem(dp + i, ND)},
            device_id_type=MESH,
        )

    for i in range(1, ND):
        to_dp(i).start()

    to_x(1, 0).wait_recv()
    to_x(1, 1).wait_recv()
    to_x(2, 0).wait_recv()
    wg_ref[:half] = acc[cx, :half] + rb2[0].astype(F32) + rb1[1].astype(F32)
    to_x(2, 1).wait_recv()
    wg_ref[half:] = acc[cx, half:] + rb1[0].astype(F32) + rb2[1].astype(F32)

    for i in range(1, ND):
        to_dp(i).wait_recv()
    total = jnp.zeros((8, 128), F32)
    for j in range(ND):
        i = lax.rem(dp - j + ND, ND)
        total = total + jnp.where(i == 0, part_s[...], parts[jnp.maximum(i - 1, 0)])
    gg_ref[...] = total[:, 0:TOK]

    @pl.loop(0, 16)
    def _(k):
        for c in range(NCH):
            hop(0, c, k).wait_send()

            @pl.when(k < 15)
            def _():
                hop(1, c, k).wait_send()

    @pl.loop(0, NG)
    def _(g):
        to_partner(g).wait_send()
        for i in range(1, 4):
            to_y(g, i).wait_send()

    @pl.loop(1, NZ)
    def _(p):
        to_home(p, zright).wait_send()

    for i in range(1, ND):
        to_dp(i).wait_send()
    for kind in range(3):
        for d in range(2):
            to_x(kind, d).wait_send()


def body(out_grad, expert_ids, gates, hidden_saved, w_down):
    any_spec = pl.BlockSpec(memory_space=pl.ANY)
    vmem = pl.BlockSpec(memory_space=pltpu.VMEM)
    half = FQ // 2
    dma = pltpu.SemaphoreType.DMA
    d_hidden, w_grad, gate_grad = pl.pallas_call(
        kernel,
        out_shape=(
            jax.ShapeDtypeStruct((NZ, CAP, SH), BF),
            jax.ShapeDtypeStruct((FQ, WID), F32),
            jax.ShapeDtypeStruct((8, TOK), F32),
        ),
        in_specs=[vmem, vmem, vmem, any_spec, any_spec],
        out_specs=[vmem, vmem, vmem],
        scratch_shapes=[
            pltpu.VMEM((NZ, ROWS, 128), BF),
            pltpu.VMEM((NZ, CAP, FF), BF),
            pltpu.VMEM((2, 4, SH, WID), BF),
            pltpu.VMEM((NC, FQ, WID), F32),
            pltpu.VMEM((GR, WID), BF),
            pltpu.VMEM((GR, WID), BF),
            pltpu.VMEM((4, GR, SH), BF),
            pltpu.VMEM((2, 128, 256), F32),
            pltpu.VMEM((GR, 1), F32),
            pltpu.VMEM((NG, 4, GR, SH), BF),
            pltpu.VMEM((NG, 4, GR, SH), BF),
            pltpu.VMEM((NG, 3, GR, SH), BF),
            pltpu.VMEM((NG, 3, GR, SH), BF),
            pltpu.VMEM((NZ // 2, 1, 128), F32),
            pltpu.VMEM((NZ, 1, 128), F32),
            pltpu.VMEM((8, 128), F32),
            pltpu.VMEM((ND - 1, 8, 128), F32),
            pltpu.VMEM((2, half, WID), BF),
            pltpu.VMEM((2, half, WID), BF),
            pltpu.VMEM((2, half, WID), BF),
            pltpu.VMEM((2, half, WID), BF),
            pltpu.VMEM((2, half, WID), BF),
            pltpu.VMEM((2, half, WID), BF),
            dma((3,)),
            dma((2, NCH, 16)),
            dma((2, NCH, 16)),
            dma((NG,)),
            dma((NG,)),
            dma((NG, 3)),
            dma((NG, 3)),
            dma((NZ,)),
            dma((NZ,)),
            dma((ND - 1,)),
            dma((ND - 1,)),
            dma((3, 2)),
            dma((3, 2)),
        ],
        compiler_params=pltpu.CompilerParams(
            collective_id=0, has_side_effects=True, vmem_limit_bytes=48 * 2**20
        ),
        cost_estimate=pl.CostEstimate(
            flops=4 * 1024 * 1024 * 896, bytes_accessed=6 * 2**20, transcendentals=0
        ),
    )(
        out_grad,
        expert_ids.T,
        gates.T,
        hidden_saved.reshape(NZ, CAP, FF),
        w_down.reshape(4, 2, SH, WID),
    )
    return (
        d_hidden.reshape(NZ * CAP, SH),
        w_grad.reshape(1, FQ, WID),
        gate_grad.T,
    )


def solution(mesh):
    return jax.shard_map(
        body,
        mesh=mesh,
        in_specs=(
            P(("ctx", "expert"), "dp"),
            P(("ctx", "expert"), None),
            P(("ctx", "expert"), None),
            P(("ctx", "expert"), None),
            P("expert", None, "dp"),
        ),
        out_specs=(
            P(("ctx", "expert"), "dp"),
            P("expert", "ctx", "dp"),
            P(("ctx", "expert"), None),
        ),
        check_vma=False,
    )
```

```python
import functools

import jax
import jax.numpy as jnp
from jax import lax
from jax.experimental import pallas as pl
from jax.experimental.pallas import tpu as pltpu
from jax.sharding import PartitionSpec as P

MESH = pl.DeviceIdType.MESH
BF = jnp.bfloat16
F32 = jnp.float32

NZ = 32
NC = 4
ND = 8
TOK = 64
CAP = 32
FF = 1024
WID = 896
TILES = WID // 128
SH = FF // ND
FQ = FF // NC
META = 16
ROWS = META + TOK * TILES
GB = 8
NG = NZ // GB
GR = GB * CAP
GT = GB * TOK
CHUNKS = ((0, META + 2 * TOK), (META + 2 * TOK, 2 * TOK), (META + 4 * TOK, 2 * TOK), (META + 6 * TOK, TOK))
NCH = len(CHUNKS)


def kernel(
    x_hbm, ids_hbm, gates_hbm, hid_hbm, w_hbm,
    dh_ref, wg_ref, gg_ref,
    gat, ids_ref, gates_ref, hid, wv, acc, rows_s, scaled_s, pown, sel_s, gcol_s, gsum,
    pbuf, prec, qbuf, qrec, gsend, gback, part_s, parts,
    xa, xb1, xb2, ra, rb1, rb2,
    load_sem, zs, zr, cs, cr, ys, yr, gs, gr, ps, pr, xs, xr,
):
    z = lax.axis_index("expert")
    dp = lax.axis_index("dp")
    cx = lax.axis_index("ctx")
    core = lax.rem(dp, 2)
    yy = dp // 2
    zright = lax.rem(z + 1, NZ)
    zleft = lax.rem(z + NZ - 1, NZ)
    cright = lax.rem(cx + 1, NC)
    cleft = lax.rem(cx + NC - 1, NC)
    copp = lax.rem(cx + 2, NC)
    partner = dp + 1 - 2 * core

    first = (
        pltpu.make_async_copy(ids_hbm, ids_ref, load_sem.at[3]),
        pltpu.make_async_copy(gates_hbm, gates_ref, load_sem.at[4]),
    )
    tiles = [
        pltpu.make_async_copy(
            x_hbm.at[:, pl.ds(j * 128, 128)],
            gat.at[0, pl.ds(META + j * TOK, TOK)],
            load_sem.at[5 + j],
        )
        for j in range(TILES)
    ]
    for load in first:
        load.start()
    for load in tiles:
        load.start()

    barrier = pltpu.get_barrier_semaphore()
    for nb in (zright, zleft):
        pl.semaphore_signal(barrier, inc=1, device_id={"expert": nb}, device_id_type=MESH)
    for nb in (cright, cleft):
        pl.semaphore_signal(barrier, inc=1, device_id={"ctx": nb}, device_id_type=MESH)
    for i in range(1, ND):
        pl.semaphore_signal(
            barrier, inc=1, device_id={"dp": lax.rem(dp + i, ND)}, device_id_type=MESH
        )

    loads = (
        pltpu.make_async_copy(hid_hbm, hid, load_sem.at[0]),
        pltpu.make_async_copy(w_hbm.at[:, core], wv.at[0], load_sem.at[1]),
        pltpu.make_async_copy(w_hbm.at[:, 1 - core], wv.at[1], load_sem.at[2]),
    )
    for load in loads:
        load.start()

    for load in first:
        load.wait()

    e_iota = lax.broadcasted_iota(jnp.int32, (NZ, TOK), 0)
    gate_tab = jnp.zeros((NZ, TOK), F32)
    gates = gates_ref[...].astype(F32)
    for k in range(8):
        gate_tab = gate_tab + jnp.where(e_iota == ids_ref[k : k + 1, :], gates[k : k + 1, :], 0.0)
    gat[0, 0:META, :] = jnp.concatenate([gate_tab[0:META], gate_tab[META:]], axis=1).astype(BF)
    for load in tiles:
        load.wait()

    pl.semaphore_wait(barrier, 4 + ND - 1)

    def hop(d, c, k):
        lo, n = CHUNKS[c]
        if d == 0:
            src, dst, dev = jnp.maximum(2 * k - 1, 0), 2 * k + 1, zright
        else:
            src, dst, dev = 2 * k, 2 * k + 2, zleft
        return pltpu.make_async_remote_copy(
            src_ref=gat.at[src, pl.ds(lo, n)],
            dst_ref=gat.at[dst, pl.ds(lo, n)],
            send_sem=zs.at[d, c, k],
            recv_sem=zr.at[d, c, k],
            device_id={"expert": dev},
            device_id_type=MESH,
        )

    for c in range(NCH):
        for d in range(2):
            hop(d, c, jnp.int32(0)).start()

    for load in loads:
        load.wait()
    acc[...] = jnp.zeros_like(acc)

    def ring_step(k, part):
        for c in (0, 1) if part == 0 else (2, 3):
            hop(0, c, k).wait_recv()

            @pl.when(k < 15)
            def _():
                hop(0, c, k + 1).start()
                hop(1, c, k).wait_recv()

            @pl.when(k < 14)
            def _():
                hop(1, c, k + 1).start()

    def source_of(g, i):
        dist = GB // 2 * g + (i + 1) // 2
        return lax.rem(z + dist if i % 2 == 0 else z - dist + NZ, NZ)

    def rows_of_group(g, h):
        base = g * GB
        lane = lax.broadcasted_iota(jnp.int32, (GB, 128), 1)
        row = lax.broadcasted_iota(jnp.int32, (GB, 128), 0)
        tab = gat[pl.ds(base, GB), 0:META, :].astype(F32)
        sub = lax.broadcasted_iota(jnp.int32, (GB, META, 128), 1)
        mine = jnp.sum(jnp.where(sub == lax.rem(z, META), tab, 0.0), axis=1)
        odd = lax.rem(row, 2)
        mine = jnp.where(odd == z // META, mine, pltpu.roll(mine, TOK, 1))
        mine = jnp.where(lane // TOK == odd, mine, 0.0)
        named = mine > 0.0
        t0 = lax.broadcasted_iota(jnp.int32, (128, 128), 0)
        t1 = lax.broadcasted_iota(jnp.int32, (128, 128), 1)
        before = jnp.where((t0 < t1) & (t0 // TOK == t1 // TOK), 1.0, 0.0).astype(BF)
        count = jnp.dot(
            jnp.where(named, 1.0, 0.0).astype(BF), before, preferred_element_type=F32
        ).astype(jnp.int32)
        target = jnp.where(named, lax.rem(row, 4) * CAP + count, -1)
        slot = lax.broadcasted_iota(jnp.int32, (128, 128), 0)
        sel, gsel = [], []
        for j in range(2):
            a = 4 * h + 2 * j
            t = jnp.maximum(target[a : a + 1], target[a + 1 : a + 2])
            gv = mine[a : a + 1] + mine[a + 1 : a + 2]
            one = slot == t
            sel.append(jnp.where(one, 1.0, 0.0))
            gsel.append(jnp.where(one, gv, 0.0))
        sel = jnp.concatenate(sel, axis=1)
        gsel = jnp.concatenate(gsel, axis=1)
        sel_s[h] = sel
        gcol_s[h * 128 : (h + 1) * 128, :] = jnp.sum(gsel, axis=1, keepdims=True)
        sel = sel.astype(BF)
        gsel = gsel.astype(BF)
        for j in range(TILES):
            xt = gat[
                pl.ds(base + 4 * h, 4), META + j * TOK : META + (j + 1) * TOK, :
            ].reshape(4 * TOK, 128)
            cols = slice(j * 128, (j + 1) * 128)
            rows_s[h * 128 : (h + 1) * 128, cols] = jnp.dot(
                sel, xt, preferred_element_type=F32
            ).astype(BF)
            scaled_s[h * 128 : (h + 1) * 128, cols] = jnp.dot(
                gsel, xt, preferred_element_type=F32
            ).astype(BF)

    def partial_of(which, y):
        return lax.dot_general(
            rows_s[...], wv[which, y], (((1,), (1,)), ((), ())), preferred_element_type=F32
        )

    def to_partner(g):
        return pltpu.make_async_remote_copy(
            src_ref=pbuf.at[g],
            dst_ref=prec.at[g],
            send_sem=cs.at[g],
            recv_sem=cr.at[g],
            device_id={"dp": partner},
            device_id_type=MESH,
        )

    def to_y(g, i):
        return pltpu.make_async_remote_copy(
            src_ref=qbuf.at[g, i - 1],
            dst_ref=qrec.at[g, i - 1],
            send_sem=ys.at[g, i - 1],
            recv_sem=yr.at[g, i - 1],
            device_id={"dp": lax.rem(dp + 2 * i, ND)},
            device_id_type=MESH,
        )

    def hidden_cols(g, unit):
        cols = pl.ds(pl.multiple_of(unit * SH, SH), SH)
        return jnp.concatenate(
            [hid[source_of(g, i), :, cols] for i in range(GB)], axis=0
        ).astype(F32)

    def send_partials(g):
        mine = jnp.zeros((GR, SH), F32)
        for y in range(4):
            part = partial_of(1, y).astype(BF)
            pbuf[g, y] = part
            mine = mine + hidden_cols(g, 2 * y + 1 - core) * part.astype(F32)
        gsum[...] = mine
        to_partner(g).start()

    def own_partials(g):
        mine = gsum[...]
        for y in range(4):
            part = partial_of(0, y).astype(BF)
            pown[y] = part
            mine = mine + hidden_cols(g, 2 * y + core) * part.astype(F32)
        col = jnp.sum(mine, axis=1, keepdims=True)
        for h in range(2):
            back = jnp.sum(sel_s[h] * col[h * 128 : (h + 1) * 128], axis=0, keepdims=True)
            for j in range(2):
                gsend[g * 4 + 2 * h + j] = back[:, j * 128 : (j + 1) * 128]
        for i in range(GB):
            p = g * GB + i
            if i == 0:

                @pl.when(g > 0)
                def _():
                    to_home(p, source_of(g, i)).start()

                @pl.when(g == 0)
                def _():
                    gback[z] = gsend[0]
            else:
                to_home(p, source_of(g, i)).start()

    def contribute(g, share):
        parts_h = [
            hid[source_of(g, i), :, pl.ds(pl.multiple_of(share * FQ, FQ), FQ)] for i in range(GB)
        ]
        acc[share] += lax.dot_general(
            jnp.concatenate(parts_h, axis=0),
            scaled_s[...],
            (((0,), (0,)), ((), ())),
            preferred_element_type=F32,
        )

    def sum_cores(g):
        to_partner(g).wait_recv()
        for i in range(1, 4):
            y = lax.rem(yy + i, 4)
            qbuf[g, i - 1] = (pown[y].astype(F32) + prec[g, y].astype(F32)).astype(BF)
            to_y(g, i).start()

    def to_home(p, s):
        return pltpu.make_async_remote_copy(
            src_ref=gsend.at[p // 2],
            dst_ref=gback.at[z],
            send_sem=gs.at[p],
            recv_sem=gr.at[z],
            device_id={"expert": s},
            device_id_type=MESH,
        )

    def finish_rows(g):
        total = pown[yy].astype(F32) + prec[g, yy].astype(F32)
        for i in range(1, 4):
            to_y(g, i).wait_recv()
            total = total + qrec[g, i - 1].astype(F32)
        dh = (gcol_s[...] * total).astype(BF)
        for i in range(GB):
            dh_ref[source_of(g, i)] = dh[i * CAP : (i + 1) * CAP]

    pieces = (
        lambda g: rows_of_group(g, 0),
        lambda g: rows_of_group(g, 1),
        send_partials,
        own_partials,
        lambda g: (sum_cores(g), contribute(g, jnp.int32(0))),
        lambda g: contribute(g, jnp.int32(1)),
        lambda g: contribute(g, jnp.int32(2)),
        lambda g: (contribute(g, jnp.int32(3)), finish_rows(g)),
    )

    @pl.loop(0, NG)
    def _(g):
        for i, piece in enumerate(pieces):
            ring_step(4 * g + i // 2, i % 2)

            @pl.when(g > 0)
            def _():
                piece(g - 1)

    half = FQ // 2

    def to_x(kind, d):
        src = (xa, xb1, xb2)[kind]
        dst = (ra, rb1, rb2)[kind]
        return pltpu.make_async_remote_copy(
            src_ref=src.at[d],
            dst_ref=dst.at[d],
            send_sem=xs.at[kind, d],
            recv_sem=xr.at[kind, d],
            device_id={"ctx": (cright, cleft)[d]},
            device_id_type=MESH,
        )

    last = jnp.int32(NG - 1)
    rows_of_group(last, 0)
    rows_of_group(last, 1)
    contribute(last, copp)
    for d in range(2):
        xa[d] = acc[copp, d * half : (d + 1) * half].astype(BF)
        to_x(0, d).start()
    send_partials(last)
    own_partials(last)
    contribute(last, cright)
    contribute(last, cleft)
    xb1[0] = acc[cright, half:].astype(BF)
    to_x(1, 0).start()
    xb1[1] = acc[cleft, :half].astype(BF)
    to_x(1, 1).start()
    sum_cores(last)
    contribute(last, cx)
    to_x(0, 0).wait_recv()
    xb2[0] = (acc[cright, :half] + ra[0].astype(F32)).astype(BF)
    to_x(2, 0).start()
    to_x(0, 1).wait_recv()
    xb2[1] = (acc[cleft, half:] + ra[1].astype(F32)).astype(BF)
    to_x(2, 1).start()
    finish_rows(last)

    def from_home(e):
        return pltpu.make_async_remote_copy(
            src_ref=gsend.at[0],
            dst_ref=gback.at[e],
            send_sem=gs.at[0],
            recv_sem=gr.at[e],
            device_id={"expert": e},
            device_id_type=MESH,
        )

    @pl.loop(1, NZ)
    def _(i):
        from_home(lax.rem(z + i, NZ)).wait_recv()

    back = gback[...].reshape(NZ, 128)
    e2 = lax.broadcasted_iota(jnp.int32, (NZ, 128), 0)
    dist = lax.rem(e2 - z + NZ, NZ)
    swap = (dist >= 1) & (dist <= NZ // 2)
    back = jnp.where(swap, pltpu.roll(back, TOK, 1), back)[:, 0:TOK]
    mine = []
    for k in range(8):
        mine.append(
            jnp.sum(jnp.where(e_iota == ids_ref[k : k + 1, :], back, 0.0), axis=0, keepdims=True)
        )
    mine = jnp.concatenate(mine, axis=0)
    part_s[...] = jnp.concatenate([mine, jnp.zeros_like(mine)], axis=1)

    def to_dp(i):
        return pltpu.make_async_remote_copy(
            src_ref=part_s,
            dst_ref=parts.at[i - 1],
            send_sem=ps.at[i - 1],
            recv_sem=pr.at[i - 1],
            device_id={"dp": lax.rem(dp + i, ND)},
            device_id_type=MESH,
        )

    for i in range(1, ND):
        to_dp(i).start()

    to_x(1, 0).wait_recv()
    to_x(1, 1).wait_recv()
    to_x(2, 0).wait_recv()
    wg_ref[:half] = acc[cx, :half] + rb2[0].astype(F32) + rb1[1].astype(F32)
    to_x(2, 1).wait_recv()
    wg_ref[half:] = acc[cx, half:] + rb1[0].astype(F32) + rb2[1].astype(F32)

    for i in range(1, ND):
        to_dp(i).wait_recv()
    total = jnp.zeros((8, 128), F32)
    for j in range(ND):
        i = lax.rem(dp - j + ND, ND)
        total = total + jnp.where(i == 0, part_s[...], parts[jnp.maximum(i - 1, 0)])
    gg_ref[...] = total[:, 0:TOK]

    @pl.loop(0, 16)
    def _(k):
        for c in range(NCH):
            hop(0, c, k).wait_send()

            @pl.when(k < 15)
            def _():
                hop(1, c, k).wait_send()

    @pl.loop(0, NG)
    def _(g):
        to_partner(g).wait_send()
        for i in range(1, 4):
            to_y(g, i).wait_send()

    @pl.loop(1, NZ)
    def _(p):
        to_home(p, zright).wait_send()

    for i in range(1, ND):
        to_dp(i).wait_send()
    for kind in range(3):
        for d in range(2):
            to_x(kind, d).wait_send()


def body(out_grad, expert_ids, gates, hidden_saved, w_down):
    any_spec = pl.BlockSpec(memory_space=pl.ANY)
    vmem = pl.BlockSpec(memory_space=pltpu.VMEM)
    half = FQ // 2
    dma = pltpu.SemaphoreType.DMA
    d_hidden, w_grad, gate_grad = pl.pallas_call(
        kernel,
        out_shape=(
            jax.ShapeDtypeStruct((NZ, CAP, SH), BF),
            jax.ShapeDtypeStruct((FQ, WID), F32),
            jax.ShapeDtypeStruct((8, TOK), F32),
        ),
        in_specs=[any_spec] * 5,
        out_specs=[vmem, vmem, vmem],
        scratch_shapes=[
            pltpu.VMEM((NZ, ROWS, 128), BF),
            pltpu.VMEM((8, TOK), jnp.int32),
            pltpu.VMEM((8, TOK), BF),
            pltpu.VMEM((NZ, CAP, FF), BF),
            pltpu.VMEM((2, 4, SH, WID), BF),
            pltpu.VMEM((NC, FQ, WID), F32),
            pltpu.VMEM((GR, WID), BF),
            pltpu.VMEM((GR, WID), BF),
            pltpu.VMEM((4, GR, SH), BF),
            pltpu.VMEM((2, 128, 256), F32),
            pltpu.VMEM((GR, 1), F32),
            pltpu.VMEM((GR, SH), F32),
            pltpu.VMEM((NG, 4, GR, SH), BF),
            pltpu.VMEM((NG, 4, GR, SH), BF),
            pltpu.VMEM((NG, 3, GR, SH), BF),
            pltpu.VMEM((NG, 3, GR, SH), BF),
            pltpu.VMEM((NZ // 2, 1, 128), F32),
            pltpu.VMEM((NZ, 1, 128), F32),
            pltpu.VMEM((8, 128), F32),
            pltpu.VMEM((ND - 1, 8, 128), F32),
            pltpu.VMEM((2, half, WID), BF),
            pltpu.VMEM((2, half, WID), BF),
            pltpu.VMEM((2, half, WID), BF),
            pltpu.VMEM((2, half, WID), BF),
            pltpu.VMEM((2, half, WID), BF),
            pltpu.VMEM((2, half, WID), BF),
            dma((5 + TILES,)),
            dma((2, NCH, 16)),
            dma((2, NCH, 16)),
            dma((NG,)),
            dma((NG,)),
            dma((NG, 3)),
            dma((NG, 3)),
            dma((NZ,)),
            dma((NZ,)),
            dma((ND - 1,)),
            dma((ND - 1,)),
            dma((3, 2)),
            dma((3, 2)),
        ],
        compiler_params=pltpu.CompilerParams(
            collective_id=0, has_side_effects=True, vmem_limit_bytes=60 * 2**20
        ),
        cost_estimate=pl.CostEstimate(
            flops=4 * 1024 * 1024 * 896, bytes_accessed=6 * 2**20, transcendentals=0
        ),
    )(
        out_grad,
        expert_ids.T,
        gates.T,
        hidden_saved.reshape(NZ, CAP, FF),
        w_down.reshape(4, 2, SH, WID),
    )
    return (
        d_hidden.reshape(NZ * CAP, SH),
        w_grad.reshape(1, FQ, WID),
        gate_grad.T,
    )


def solution(mesh):
    return jax.shard_map(
        body,
        mesh=mesh,
        in_specs=(
            P(("ctx", "expert"), "dp"),
            P(("ctx", "expert"), None),
            P(("ctx", "expert"), None),
            P(("ctx", "expert"), None),
            P("expert", None, "dp"),
        ),
        out_specs=(
            P(("ctx", "expert"), "dp"),
            P("expert", "ctx", "dp"),
            P(("ctx", "expert"), None),
        ),
        check_vma=False,
    )
```

```python
import functools

import jax
import jax.numpy as jnp
from jax import lax
from jax.experimental import pallas as pl
from jax.experimental.pallas import tpu as pltpu
from jax.sharding import PartitionSpec as P

MESH = pl.DeviceIdType.MESH
BF = jnp.bfloat16
F32 = jnp.float32

NZ = 32
NC = 4
ND = 8
TOK = 64
CAP = 32
FF = 1024
WID = 896
TILES = WID // 128
SH = FF // ND
FQ = FF // NC
META = 16
ROWS = META + TOK * TILES
GB = 8
NG = NZ // GB
GR = GB * CAP
GT = GB * TOK
CHUNKS = ((0, META + TOK), (META + TOK, 2 * TOK), (META + 3 * TOK, 2 * TOK), (META + 5 * TOK, 2 * TOK))
NCH = len(CHUNKS)


def kernel(
    x_hbm, ids_hbm, gates_hbm, hid_hbm, w_hbm,
    dh_ref, wg_ref, gg_ref,
    gat, ids_ref, gates_ref, hid, wv, acc, rows_s, scaled_s, pown, sel_s, gcol_s, gsum,
    pbuf, prec, qbuf, qrec, gsend, gback, part_s, parts,
    xa, xb1, xb2, ra, rb1, rb2,
    load_sem, zs, zr, cs, cr, ys, yr, gs, gr, ps, pr, xs, xr,
):
    z = lax.axis_index("expert")
    dp = lax.axis_index("dp")
    cx = lax.axis_index("ctx")
    core = lax.rem(dp, 2)
    yy = dp // 2
    zright = lax.rem(z + 1, NZ)
    zleft = lax.rem(z + NZ - 1, NZ)
    cright = lax.rem(cx + 1, NC)
    cleft = lax.rem(cx + NC - 1, NC)
    copp = lax.rem(cx + 2, NC)
    partner = dp + 1 - 2 * core

    first = (
        pltpu.make_async_copy(ids_hbm, ids_ref, load_sem.at[3]),
        pltpu.make_async_copy(gates_hbm, gates_ref, load_sem.at[4]),
    )
    tiles = [
        pltpu.make_async_copy(
            x_hbm.at[:, pl.ds(j * 128, 128)],
            gat.at[0, pl.ds(META + j * TOK, TOK)],
            load_sem.at[5 + j],
        )
        for j in range(TILES)
    ]
    for load in first:
        load.start()
    for load in tiles:
        load.start()

    barrier = pltpu.get_barrier_semaphore()
    for nb in (zright, zleft):
        pl.semaphore_signal(barrier, inc=1, device_id={"expert": nb}, device_id_type=MESH)
    for nb in (cright, cleft):
        pl.semaphore_signal(barrier, inc=1, device_id={"ctx": nb}, device_id_type=MESH)
    for i in range(1, ND):
        pl.semaphore_signal(
            barrier, inc=1, device_id={"dp": lax.rem(dp + i, ND)}, device_id_type=MESH
        )

    loads = (
        pltpu.make_async_copy(hid_hbm, hid, load_sem.at[0]),
        pltpu.make_async_copy(w_hbm.at[:, core], wv.at[0], load_sem.at[1]),
        pltpu.make_async_copy(w_hbm.at[:, 1 - core], wv.at[1], load_sem.at[2]),
    )
    for load in loads:
        load.start()

    for load in first:
        load.wait()

    e_iota = lax.broadcasted_iota(jnp.int32, (NZ, TOK), 0)
    gate_tab = jnp.zeros((NZ, TOK), F32)
    gates = gates_ref[...].astype(F32)
    for k in range(8):
        gate_tab = gate_tab + jnp.where(e_iota == ids_ref[k : k + 1, :], gates[k : k + 1, :], 0.0)
    gat[0, 0:META, :] = jnp.concatenate([gate_tab[0:META], gate_tab[META:]], axis=1).astype(BF)
    for load in tiles:
        load.wait()

    pl.semaphore_wait(barrier, 4 + ND - 1)

    def hop(d, c, k):
        lo, n = CHUNKS[c]
        if d == 0:
            src, dst, dev = jnp.maximum(2 * k - 1, 0), 2 * k + 1, zright
        else:
            src, dst, dev = 2 * k, jnp.minimum(2 * k + 2, NZ - 1), zleft
        return pltpu.make_async_remote_copy(
            src_ref=gat.at[src, pl.ds(lo, n)],
            dst_ref=gat.at[dst, pl.ds(lo, n)],
            send_sem=zs.at[d, c, k],
            recv_sem=zr.at[d, c, k],
            device_id={"expert": dev},
            device_id_type=MESH,
        )

    for c in range(NCH):
        for d in range(2):
            hop(d, c, jnp.int32(0)).start()

    for load in loads:
        load.wait()
    acc[...] = jnp.zeros_like(acc)

    def ring_step(k, part):
        for c in (0, 1) if part == 0 else (2, 3):
            for d in range(2):
                hops = 16 if c // 2 == d else 15

                @pl.when(k < hops)
                def _():
                    hop(d, c, k).wait_recv()

                @pl.when(k < hops - 1)
                def _():
                    hop(d, c, k + 1).start()

    def source_of(g, i):
        dist = GB // 2 * g + (i + 1) // 2
        return lax.rem(z + dist if i % 2 == 0 else z - dist + NZ, NZ)

    def rows_of_group(g, h):
        base = g * GB
        lane = lax.broadcasted_iota(jnp.int32, (GB, 128), 1)
        row = lax.broadcasted_iota(jnp.int32, (GB, 128), 0)
        tab = gat[pl.ds(base, GB), 0:META, :].astype(F32)
        sub = lax.broadcasted_iota(jnp.int32, (GB, META, 128), 1)
        mine = jnp.sum(jnp.where(sub == lax.rem(z, META), tab, 0.0), axis=1)
        odd = lax.rem(row, 2)
        mine = jnp.where(odd == z // META, mine, pltpu.roll(mine, TOK, 1))
        mine = jnp.where(lane // TOK == odd, mine, 0.0)
        named = mine > 0.0
        t0 = lax.broadcasted_iota(jnp.int32, (128, 128), 0)
        t1 = lax.broadcasted_iota(jnp.int32, (128, 128), 1)
        before = jnp.where((t0 < t1) & (t0 // TOK == t1 // TOK), 1.0, 0.0).astype(BF)
        count = jnp.dot(
            jnp.where(named, 1.0, 0.0).astype(BF), before, preferred_element_type=F32
        ).astype(jnp.int32)
        target = jnp.where(named, lax.rem(row, 4) * CAP + count, -1)
        slot = lax.broadcasted_iota(jnp.int32, (128, 128), 0)
        sel, gsel = [], []
        for j in range(2):
            a = 4 * h + 2 * j
            t = jnp.maximum(target[a : a + 1], target[a + 1 : a + 2])
            gv = mine[a : a + 1] + mine[a + 1 : a + 2]
            one = slot == t
            sel.append(jnp.where(one, 1.0, 0.0))
            gsel.append(jnp.where(one, gv, 0.0))
        sel = jnp.concatenate(sel, axis=1)
        gsel = jnp.concatenate(gsel, axis=1)
        sel_s[h] = sel
        gcol_s[h * 128 : (h + 1) * 128, :] = jnp.sum(gsel, axis=1, keepdims=True)
        sel = sel.astype(BF)
        gsel = gsel.astype(BF)
        for j in range(TILES):
            xt = gat[
                pl.ds(base + 4 * h, 4), META + j * TOK : META + (j + 1) * TOK, :
            ].reshape(4 * TOK, 128)
            cols = slice(j * 128, (j + 1) * 128)
            rows_s[h * 128 : (h + 1) * 128, cols] = jnp.dot(
                sel, xt, preferred_element_type=F32
            ).astype(BF)
            scaled_s[h * 128 : (h + 1) * 128, cols] = jnp.dot(
                gsel, xt, preferred_element_type=F32
            ).astype(BF)

    def partial_of(which, y):
        return lax.dot_general(
            rows_s[...], wv[which, y], (((1,), (1,)), ((), ())), preferred_element_type=F32
        )

    def to_partner(g):
        return pltpu.make_async_remote_copy(
            src_ref=pbuf.at[g],
            dst_ref=prec.at[g],
            send_sem=cs.at[g],
            recv_sem=cr.at[g],
            device_id={"dp": partner},
            device_id_type=MESH,
        )

    def to_y(g, i):
        return pltpu.make_async_remote_copy(
            src_ref=qbuf.at[g, i - 1],
            dst_ref=qrec.at[g, i - 1],
            send_sem=ys.at[g, i - 1],
            recv_sem=yr.at[g, i - 1],
            device_id={"dp": lax.rem(dp + 2 * i, ND)},
            device_id_type=MESH,
        )

    def hidden_cols(g, unit):
        cols = pl.ds(pl.multiple_of(unit * SH, SH), SH)
        return jnp.concatenate(
            [hid[source_of(g, i), :, cols] for i in range(GB)], axis=0
        ).astype(F32)

    def send_partials(g):
        mine = jnp.zeros((GR, SH), F32)
        for y in range(4):
            part = partial_of(1, y).astype(BF)
            pbuf[g, y] = part
            mine = mine + hidden_cols(g, 2 * y + 1 - core) * part.astype(F32)
        gsum[...] = mine
        to_partner(g).start()

    def own_partials(g):
        mine = gsum[...]
        for y in range(4):
            part = partial_of(0, y).astype(BF)
            pown[y] = part
            mine = mine + hidden_cols(g, 2 * y + core) * part.astype(F32)
        col = jnp.sum(mine, axis=1, keepdims=True)
        for h in range(2):
            back = jnp.sum(sel_s[h] * col[h * 128 : (h + 1) * 128], axis=0, keepdims=True)
            for j in range(2):
                gsend[g * 4 + 2 * h + j] = back[:, j * 128 : (j + 1) * 128]
        for i in range(GB):
            p = g * GB + i
            if i == 0:

                @pl.when(g > 0)
                def _():
                    to_home(p, source_of(g, i)).start()

                @pl.when(g == 0)
                def _():
                    gback[z] = gsend[0]
            else:
                to_home(p, source_of(g, i)).start()

    def contribute(g, share):
        parts_h = [
            hid[source_of(g, i), :, pl.ds(pl.multiple_of(share * FQ, FQ), FQ)] for i in range(GB)
        ]
        acc[share] += lax.dot_general(
            jnp.concatenate(parts_h, axis=0),
            scaled_s[...],
            (((0,), (0,)), ((), ())),
            preferred_element_type=F32,
        )

    def sum_cores(g):
        to_partner(g).wait_recv()
        for i in range(1, 4):
            y = lax.rem(yy + i, 4)
            qbuf[g, i - 1] = (pown[y].astype(F32) + prec[g, y].astype(F32)).astype(BF)
            to_y(g, i).start()

    def to_home(p, s):
        return pltpu.make_async_remote_copy(
            src_ref=gsend.at[p // 2],
            dst_ref=gback.at[z],
            send_sem=gs.at[p],
            recv_sem=gr.at[z],
            device_id={"expert": s},
            device_id_type=MESH,
        )

    def finish_rows(g):
        total = pown[yy].astype(F32) + prec[g, yy].astype(F32)
        for i in range(1, 4):
            to_y(g, i).wait_recv()
            total = total + qrec[g, i - 1].astype(F32)
        dh = (gcol_s[...] * total).astype(BF)
        for i in range(GB):
            dh_ref[source_of(g, i)] = dh[i * CAP : (i + 1) * CAP]

    pieces = (
        lambda g: rows_of_group(g, 0),
        lambda g: rows_of_group(g, 1),
        send_partials,
        own_partials,
        lambda g: (sum_cores(g), contribute(g, jnp.int32(0))),
        lambda g: contribute(g, jnp.int32(1)),
        lambda g: contribute(g, jnp.int32(2)),
        lambda g: (contribute(g, jnp.int32(3)), finish_rows(g)),
    )

    @pl.loop(0, NG)
    def _(g):
        for i, piece in enumerate(pieces):
            ring_step(4 * g + i // 2, i % 2)

            @pl.when(g > 0)
            def _():
                piece(g - 1)

    half = FQ // 2

    def to_x(kind, d):
        src = (xa, xb1, xb2)[kind]
        dst = (ra, rb1, rb2)[kind]
        return pltpu.make_async_remote_copy(
            src_ref=src.at[d],
            dst_ref=dst.at[d],
            send_sem=xs.at[kind, d],
            recv_sem=xr.at[kind, d],
            device_id={"ctx": (cright, cleft)[d]},
            device_id_type=MESH,
        )

    last = jnp.int32(NG - 1)
    rows_of_group(last, 0)
    rows_of_group(last, 1)
    contribute(last, copp)
    for d in range(2):
        xa[d] = acc[copp, d * half : (d + 1) * half].astype(BF)
        to_x(0, d).start()
    send_partials(last)
    own_partials(last)
    contribute(last, cright)
    contribute(last, cleft)
    xb1[0] = acc[cright, half:].astype(BF)
    to_x(1, 0).start()
    xb1[1] = acc[cleft, :half].astype(BF)
    to_x(1, 1).start()
    sum_cores(last)
    contribute(last, cx)
    to_x(0, 0).wait_recv()
    xb2[0] = (acc[cright, :half] + ra[0].astype(F32)).astype(BF)
    to_x(2, 0).start()
    to_x(0, 1).wait_recv()
    xb2[1] = (acc[cleft, half:] + ra[1].astype(F32)).astype(BF)
    to_x(2, 1).start()
    finish_rows(last)

    def from_home(e):
        return pltpu.make_async_remote_copy(
            src_ref=gsend.at[0],
            dst_ref=gback.at[e],
            send_sem=gs.at[0],
            recv_sem=gr.at[e],
            device_id={"expert": e},
            device_id_type=MESH,
        )

    @pl.loop(1, NZ)
    def _(i):
        from_home(lax.rem(z + i, NZ)).wait_recv()

    back = gback[...].reshape(NZ, 128)
    e2 = lax.broadcasted_iota(jnp.int32, (NZ, 128), 0)
    dist = lax.rem(e2 - z + NZ, NZ)
    swap = (dist >= 1) & (dist <= NZ // 2)
    back = jnp.where(swap, pltpu.roll(back, TOK, 1), back)[:, 0:TOK]
    mine = []
    for k in range(8):
        mine.append(
            jnp.sum(jnp.where(e_iota == ids_ref[k : k + 1, :], back, 0.0), axis=0, keepdims=True)
        )
    mine = jnp.concatenate(mine, axis=0)
    part_s[...] = jnp.concatenate([mine, jnp.zeros_like(mine)], axis=1)

    def to_dp(i):
        return pltpu.make_async_remote_copy(
            src_ref=part_s,
            dst_ref=parts.at[i - 1],
            send_sem=ps.at[i - 1],
            recv_sem=pr.at[i - 1],
            device_id={"dp": lax.rem(dp + i, ND)},
            device_id_type=MESH,
        )

    for i in range(1, ND):
        to_dp(i).start()

    to_x(1, 0).wait_recv()
    to_x(1, 1).wait_recv()
    to_x(2, 0).wait_recv()
    wg_ref[:half] = acc[cx, :half] + rb2[0].astype(F32) + rb1[1].astype(F32)
    to_x(2, 1).wait_recv()
    wg_ref[half:] = acc[cx, half:] + rb1[0].astype(F32) + rb2[1].astype(F32)

    for i in range(1, ND):
        to_dp(i).wait_recv()
    total = jnp.zeros((8, 128), F32)
    for j in range(ND):
        i = lax.rem(dp - j + ND, ND)
        total = total + jnp.where(i == 0, part_s[...], parts[jnp.maximum(i - 1, 0)])
    gg_ref[...] = total[:, 0:TOK]

    @pl.loop(0, 16)
    def _(k):
        for c in range(NCH):
            for d in range(2):
                hops = 16 if c // 2 == d else 15

                @pl.when(k < hops)
                def _():
                    hop(d, c, k).wait_send()

    @pl.loop(0, NG)
    def _(g):
        to_partner(g).wait_send()
        for i in range(1, 4):
            to_y(g, i).wait_send()

    @pl.loop(1, NZ)
    def _(p):
        to_home(p, zright).wait_send()

    for i in range(1, ND):
        to_dp(i).wait_send()
    for kind in range(3):
        for d in range(2):
            to_x(kind, d).wait_send()


def body(out_grad, expert_ids, gates, hidden_saved, w_down):
    any_spec = pl.BlockSpec(memory_space=pl.ANY)
    vmem = pl.BlockSpec(memory_space=pltpu.VMEM)
    half = FQ // 2
    dma = pltpu.SemaphoreType.DMA
    d_hidden, w_grad, gate_grad = pl.pallas_call(
        kernel,
        out_shape=(
            pltpu.VMEM((NZ, CAP, SH), BF),
            pltpu.VMEM((FQ, WID), F32),
            pltpu.VMEM((8, TOK), F32),
        ),
        in_specs=[any_spec] * 5,
        out_specs=[vmem, vmem, vmem],
        scratch_shapes=[
            pltpu.VMEM((NZ, ROWS, 128), BF),
            pltpu.VMEM((8, TOK), jnp.int32),
            pltpu.VMEM((8, TOK), BF),
            pltpu.VMEM((NZ, CAP, FF), BF),
            pltpu.VMEM((2, 4, SH, WID), BF),
            pltpu.VMEM((NC, FQ, WID), F32),
            pltpu.VMEM((GR, WID), BF),
            pltpu.VMEM((GR, WID), BF),
            pltpu.VMEM((4, GR, SH), BF),
            pltpu.VMEM((2, 128, 256), F32),
            pltpu.VMEM((GR, 1), F32),
            pltpu.VMEM((GR, SH), F32),
            pltpu.VMEM((NG, 4, GR, SH), BF),
            pltpu.VMEM((NG, 4, GR, SH), BF),
            pltpu.VMEM((NG, 3, GR, SH), BF),
            pltpu.VMEM((NG, 3, GR, SH), BF),
            pltpu.VMEM((NZ // 2, 1, 128), F32),
            pltpu.VMEM((NZ, 1, 128), F32),
            pltpu.VMEM((8, 128), F32),
            pltpu.VMEM((ND - 1, 8, 128), F32),
            pltpu.VMEM((2, half, WID), BF),
            pltpu.VMEM((2, half, WID), BF),
            pltpu.VMEM((2, half, WID), BF),
            pltpu.VMEM((2, half, WID), BF),
            pltpu.VMEM((2, half, WID), BF),
            pltpu.VMEM((2, half, WID), BF),
            dma((5 + TILES,)),
            dma((2, NCH, 16)),
            dma((2, NCH, 16)),
            dma((NG,)),
            dma((NG,)),
            dma((NG, 3)),
            dma((NG, 3)),
            dma((NZ,)),
            dma((NZ,)),
            dma((ND - 1,)),
            dma((ND - 1,)),
            dma((3, 2)),
            dma((3, 2)),
        ],
        compiler_params=pltpu.CompilerParams(
            collective_id=0, has_side_effects=True, vmem_limit_bytes=60 * 2**20
        ),
        cost_estimate=pl.CostEstimate(
            flops=4 * 1024 * 1024 * 896, bytes_accessed=6 * 2**20, transcendentals=0
        ),
    )(
        out_grad,
        expert_ids.T,
        gates.T,
        hidden_saved.reshape(NZ, CAP, FF),
        w_down.reshape(4, 2, SH, WID),
    )
    return (
        d_hidden.reshape(NZ * CAP, SH),
        w_grad.reshape(1, FQ, WID),
        gate_grad.T,
    )


def solution(mesh):
    return jax.shard_map(
        body,
        mesh=mesh,
        in_specs=(
            P(("ctx", "expert"), "dp"),
            P(("ctx", "expert"), None),
            P(("ctx", "expert"), None),
            P(("ctx", "expert"), None),
            P("expert", None, "dp"),
        ),
        out_specs=(
            P(("ctx", "expert"), "dp"),
            P("expert", "ctx", "dp"),
            P(("ctx", "expert"), None),
        ),
        check_vma=False,
    )
```

```python
import functools

import jax
import jax.numpy as jnp
from jax import lax
from jax.experimental import pallas as pl
from jax.experimental.pallas import tpu as pltpu
from jax.sharding import PartitionSpec as P

MESH = pl.DeviceIdType.MESH
BF = jnp.bfloat16
F32 = jnp.float32

NZ = 32
NC = 4
ND = 8
TOK = 64
CAP = 32
FF = 1024
WID = 896
TILES = WID // 128
SH = FF // ND
FQ = FF // NC
META = 16
ROWS = META + TOK * TILES
GB = 8
NG = NZ // GB
GR = GB * CAP
GT = GB * TOK
CHUNKS = ((0, META + TOK), (META + TOK, 2 * TOK), (META + 3 * TOK, 2 * TOK), (META + 5 * TOK, 2 * TOK))
NCH = len(CHUNKS)


def kernel(
    x_hbm, ids_hbm, gates_hbm, hid_hbm, w_hbm,
    dh_ref, wg_ref, gg_ref,
    gat, ids_ref, gates_ref, hid, wv, acc, rows_s, scaled_s, pown, sel_s, gcol_s, gsum,
    pbuf, prec, qbuf, qrec, gsend, gback, part_s, parts,
    xa, xb1, xb2, ra, rb1, rb2,
    load_sem, zs, zr, cs, cr, ys, yr, gs, gr, ps, pr, xs, xr,
):
    z = lax.axis_index("expert")
    dp = lax.axis_index("dp")
    cx = lax.axis_index("ctx")
    core = lax.rem(dp, 2)
    yy = dp // 2
    zright = lax.rem(z + 1, NZ)
    zleft = lax.rem(z + NZ - 1, NZ)
    cright = lax.rem(cx + 1, NC)
    cleft = lax.rem(cx + NC - 1, NC)
    copp = lax.rem(cx + 2, NC)
    partner = dp + 1 - 2 * core

    first = (
        pltpu.make_async_copy(ids_hbm, ids_ref, load_sem.at[3]),
        pltpu.make_async_copy(gates_hbm, gates_ref, load_sem.at[4]),
    )
    tiles = [
        pltpu.make_async_copy(
            x_hbm.at[:, pl.ds(j * 128, 128)],
            gat.at[0, pl.ds(META + j * TOK, TOK)],
            load_sem.at[5 + j],
        )
        for j in range(TILES)
    ]
    for load in first:
        load.start()
    for load in tiles:
        load.start()

    barrier = pltpu.get_barrier_semaphore()
    for nb in (zright, zleft):
        pl.semaphore_signal(barrier, inc=1, device_id={"expert": nb}, device_id_type=MESH)
    for nb in (cright, cleft):
        pl.semaphore_signal(barrier, inc=1, device_id={"ctx": nb}, device_id_type=MESH)
    for i in range(1, ND):
        pl.semaphore_signal(
            barrier, inc=1, device_id={"dp": lax.rem(dp + i, ND)}, device_id_type=MESH
        )

    loads = (
        pltpu.make_async_copy(hid_hbm, hid, load_sem.at[0]),
        pltpu.make_async_copy(w_hbm.at[:, core], wv.at[0], load_sem.at[1]),
        pltpu.make_async_copy(w_hbm.at[:, 1 - core], wv.at[1], load_sem.at[2]),
    )
    for load in loads:
        load.start()

    for load in first:
        load.wait()

    e_iota = lax.broadcasted_iota(jnp.int32, (NZ, TOK), 0)
    gate_tab = jnp.zeros((NZ, TOK), F32)
    gates = gates_ref[...].astype(F32)
    for k in range(8):
        gate_tab = gate_tab + jnp.where(e_iota == ids_ref[k : k + 1, :], gates[k : k + 1, :], 0.0)
    gat[0, 0:META, :] = jnp.concatenate([gate_tab[0:META], gate_tab[META:]], axis=1).astype(BF)
    for load in tiles:
        load.wait()

    pl.semaphore_wait(barrier, 4 + ND - 1)

    def hop(d, c, k):
        lo, n = CHUNKS[c]
        if d == 0:
            src, dst, dev = jnp.maximum(2 * k - 1, 0), 2 * k + 1, zright
        else:
            src, dst, dev = 2 * k, jnp.minimum(2 * k + 2, NZ - 1), zleft
        return pltpu.make_async_remote_copy(
            src_ref=gat.at[src, pl.ds(lo, n)],
            dst_ref=gat.at[dst, pl.ds(lo, n)],
            send_sem=zs.at[d, c, k],
            recv_sem=zr.at[d, c, k],
            device_id={"expert": dev},
            device_id_type=MESH,
        )

    for c in range(NCH):
        for d in range(2):
            hop(d, c, jnp.int32(0)).start()

    for load in loads:
        load.wait()
    acc[...] = jnp.zeros_like(acc)

    def ring_step(k, part):
        for c in (0, 1) if part == 0 else (2, 3):
            for d in range(2):
                hops = 16 if c // 2 == d else 15

                @pl.when(k < hops)
                def _():
                    hop(d, c, k).wait_recv()

                @pl.when(k < hops - 1)
                def _():
                    hop(d, c, k + 1).start()

    def source_of(g, i):
        dist = GB // 2 * g + (i + 1) // 2
        return lax.rem(z + dist if i % 2 == 0 else z - dist + NZ, NZ)

    def rows_of_group(g, h):
        base = g * GB
        lane = lax.broadcasted_iota(jnp.int32, (GB, 128), 1)
        row = lax.broadcasted_iota(jnp.int32, (GB, 128), 0)
        tab = gat[pl.ds(base + 4 * h, 4), 0:META, :].astype(F32)
        sub = lax.broadcasted_iota(jnp.int32, (4, META, 128), 1)
        mine = jnp.sum(jnp.where(sub == lax.rem(z, META), tab, 0.0), axis=1)
        mine = jnp.concatenate([mine, mine], axis=0)
        odd = lax.rem(row, 2)
        mine = jnp.where(odd == z // META, mine, pltpu.roll(mine, TOK, 1))
        mine = jnp.where(lane // TOK == odd, mine, 0.0)
        named = mine > 0.0
        t0 = lax.broadcasted_iota(jnp.int32, (128, 128), 0)
        t1 = lax.broadcasted_iota(jnp.int32, (128, 128), 1)
        before = jnp.where((t0 < t1) & (t0 // TOK == t1 // TOK), 1.0, 0.0).astype(BF)
        count = jnp.dot(
            jnp.where(named, 1.0, 0.0).astype(BF), before, preferred_element_type=F32
        ).astype(jnp.int32)
        target = jnp.where(named, lax.rem(row, 4) * CAP + count, -1)
        slot = lax.broadcasted_iota(jnp.int32, (128, 128), 0)
        sel, gsel = [], []
        for j in range(2):
            a = 2 * j
            t = jnp.maximum(target[a : a + 1], target[a + 1 : a + 2])
            gv = mine[a : a + 1] + mine[a + 1 : a + 2]
            one = slot == t
            sel.append(jnp.where(one, 1.0, 0.0))
            gsel.append(jnp.where(one, gv, 0.0))
        sel = jnp.concatenate(sel, axis=1)
        gsel = jnp.concatenate(gsel, axis=1)
        sel_s[h] = sel
        gcol_s[h * 128 : (h + 1) * 128, :] = jnp.sum(gsel, axis=1, keepdims=True)
        sel = sel.astype(BF)
        gsel = gsel.astype(BF)
        for j in range(TILES):
            xt = gat[
                pl.ds(base + 4 * h, 4), META + j * TOK : META + (j + 1) * TOK, :
            ].reshape(4 * TOK, 128)
            cols = slice(j * 128, (j + 1) * 128)
            rows_s[h * 128 : (h + 1) * 128, cols] = jnp.dot(
                sel, xt, preferred_element_type=F32
            ).astype(BF)
            scaled_s[h * 128 : (h + 1) * 128, cols] = jnp.dot(
                gsel, xt, preferred_element_type=F32
            ).astype(BF)

    def partial_of(which, y):
        return lax.dot_general(
            rows_s[...], wv[which, y], (((1,), (1,)), ((), ())), preferred_element_type=F32
        )

    def to_partner(g):
        return pltpu.make_async_remote_copy(
            src_ref=pbuf.at[g],
            dst_ref=prec.at[g],
            send_sem=cs.at[g],
            recv_sem=cr.at[g],
            device_id={"dp": partner},
            device_id_type=MESH,
        )

    def to_y(g, i):
        return pltpu.make_async_remote_copy(
            src_ref=qbuf.at[g, i - 1],
            dst_ref=qrec.at[g, i - 1],
            send_sem=ys.at[g, i - 1],
            recv_sem=yr.at[g, i - 1],
            device_id={"dp": lax.rem(dp + 2 * i, ND)},
            device_id_type=MESH,
        )

    def hidden_cols(g, unit):
        cols = pl.ds(pl.multiple_of(unit * SH, SH), SH)
        return jnp.concatenate(
            [hid[source_of(g, i), :, cols] for i in range(GB)], axis=0
        ).astype(F32)

    def send_partials(g):
        mine = jnp.zeros((GR, SH), F32)
        for y in range(4):
            part = partial_of(1, y).astype(BF)
            pbuf[g, y] = part
            mine = mine + hidden_cols(g, 2 * y + 1 - core) * part.astype(F32)
        gsum[...] = mine
        to_partner(g).start()

    def own_partials(g):
        mine = gsum[...]
        for y in range(4):
            part = partial_of(0, y).astype(BF)
            pown[y] = part
            mine = mine + hidden_cols(g, 2 * y + core) * part.astype(F32)
        col = jnp.sum(mine, axis=1, keepdims=True)
        for h in range(2):
            back = jnp.sum(sel_s[h] * col[h * 128 : (h + 1) * 128], axis=0, keepdims=True)
            for j in range(2):
                gsend[g * 4 + 2 * h + j] = back[:, j * 128 : (j + 1) * 128]
        for i in range(GB):
            p = g * GB + i
            if i == 0:

                @pl.when(g > 0)
                def _():
                    to_home(p, source_of(g, i)).start()

                @pl.when(g == 0)
                def _():
                    gback[z] = gsend[0]
            else:
                to_home(p, source_of(g, i)).start()

    def contribute(g, share):
        parts_h = [
            hid[source_of(g, i), :, pl.ds(pl.multiple_of(share * FQ, FQ), FQ)] for i in range(GB)
        ]
        acc[share] += lax.dot_general(
            jnp.concatenate(parts_h, axis=0),
            scaled_s[...],
            (((0,), (0,)), ((), ())),
            preferred_element_type=F32,
        )

    def sum_cores(g):
        to_partner(g).wait_recv()
        for i in range(1, 4):
            y = lax.rem(yy + i, 4)
            qbuf[g, i - 1] = (pown[y].astype(F32) + prec[g, y].astype(F32)).astype(BF)
            to_y(g, i).start()

    def to_home(p, s):
        return pltpu.make_async_remote_copy(
            src_ref=gsend.at[p // 2],
            dst_ref=gback.at[z],
            send_sem=gs.at[p],
            recv_sem=gr.at[z],
            device_id={"expert": s},
            device_id_type=MESH,
        )

    def finish_rows(g):
        total = pown[yy].astype(F32) + prec[g, yy].astype(F32)
        for i in range(1, 4):
            to_y(g, i).wait_recv()
            total = total + qrec[g, i - 1].astype(F32)
        dh = (gcol_s[...] * total).astype(BF)
        for i in range(GB):
            dh_ref[source_of(g, i)] = dh[i * CAP : (i + 1) * CAP]

    pieces = (
        lambda g: rows_of_group(g, 0),
        lambda g: rows_of_group(g, 1),
        send_partials,
        own_partials,
        lambda g: (sum_cores(g), contribute(g, jnp.int32(0))),
        lambda g: contribute(g, jnp.int32(1)),
        lambda g: contribute(g, jnp.int32(2)),
        lambda g: (contribute(g, jnp.int32(3)), finish_rows(g)),
    )

    @pl.loop(0, NG)
    def _(g):
        for i, piece in enumerate(pieces):
            if i < 6:
                ring_step(4 * g + i // 2, i % 2)
            else:

                @pl.when(g < NG - 1)
                def _():
                    ring_step(4 * g + 3, i % 2)

            @pl.when(g > 0)
            def _():
                piece(g - 1)

    half = FQ // 2

    def to_x(kind, d):
        src = (xa, xb1, xb2)[kind]
        dst = (ra, rb1, rb2)[kind]
        return pltpu.make_async_remote_copy(
            src_ref=src.at[d],
            dst_ref=dst.at[d],
            send_sem=xs.at[kind, d],
            recv_sem=xr.at[kind, d],
            device_id={"ctx": (cright, cleft)[d]},
            device_id_type=MESH,
        )

    last = jnp.int32(NG - 1)
    rows_of_group(last, 0)
    for part in range(2):
        ring_step(jnp.int32(15), part)
    rows_of_group(last, 1)
    contribute(last, copp)
    for d in range(2):
        xa[d] = acc[copp, d * half : (d + 1) * half].astype(BF)
        to_x(0, d).start()
    send_partials(last)
    own_partials(last)
    contribute(last, cright)
    contribute(last, cleft)
    xb1[0] = acc[cright, half:].astype(BF)
    to_x(1, 0).start()
    xb1[1] = acc[cleft, :half].astype(BF)
    to_x(1, 1).start()
    sum_cores(last)
    contribute(last, cx)
    to_x(0, 0).wait_recv()
    xb2[0] = (acc[cright, :half] + ra[0].astype(F32)).astype(BF)
    to_x(2, 0).start()
    to_x(0, 1).wait_recv()
    xb2[1] = (acc[cleft, half:] + ra[1].astype(F32)).astype(BF)
    to_x(2, 1).start()

    @pl.loop(0, 16)
    def _(k):
        for c in range(NCH):
            for d in range(2):
                hops = 16 if c // 2 == d else 15

                @pl.when(k < hops)
                def _():
                    hop(d, c, k).wait_send()

    finish_rows(last)

    def from_home(e):
        return pltpu.make_async_remote_copy(
            src_ref=gsend.at[0],
            dst_ref=gback.at[e],
            send_sem=gs.at[0],
            recv_sem=gr.at[e],
            device_id={"expert": e},
            device_id_type=MESH,
        )

    @pl.loop(1, NZ)
    def _(i):
        from_home(lax.rem(z + i, NZ)).wait_recv()

    back = gback[...].reshape(NZ, 128)
    e2 = lax.broadcasted_iota(jnp.int32, (NZ, 128), 0)
    dist = lax.rem(e2 - z + NZ, NZ)
    swap = (dist >= 1) & (dist <= NZ // 2)
    back = jnp.where(swap, pltpu.roll(back, TOK, 1), back)[:, 0:TOK]
    mine = []
    for k in range(8):
        mine.append(
            jnp.sum(jnp.where(e_iota == ids_ref[k : k + 1, :], back, 0.0), axis=0, keepdims=True)
        )
    mine = jnp.concatenate(mine, axis=0)
    part_s[...] = jnp.concatenate([mine, jnp.zeros_like(mine)], axis=1)

    def to_dp(i):
        return pltpu.make_async_remote_copy(
            src_ref=part_s,
            dst_ref=parts.at[i - 1],
            send_sem=ps.at[i - 1],
            recv_sem=pr.at[i - 1],
            device_id={"dp": lax.rem(dp + i, ND)},
            device_id_type=MESH,
        )

    for i in range(1, ND):
        to_dp(i).start()

    @pl.loop(0, NG)
    def _(g):
        to_partner(g).wait_send()
        for i in range(1, 4):
            to_y(g, i).wait_send()

    @pl.loop(1, NZ)
    def _(p):
        to_home(p, zright).wait_send()

    to_x(1, 0).wait_recv()
    to_x(1, 1).wait_recv()
    to_x(2, 0).wait_recv()
    wg_ref[:half] = acc[cx, :half] + rb2[0].astype(F32) + rb1[1].astype(F32)
    to_x(2, 1).wait_recv()
    wg_ref[half:] = acc[cx, half:] + rb1[0].astype(F32) + rb2[1].astype(F32)

    for i in range(1, ND):
        to_dp(i).wait_recv()
    total = jnp.zeros((8, 128), F32)
    for j in range(ND):
        i = lax.rem(dp - j + ND, ND)
        total = total + jnp.where(i == 0, part_s[...], parts[jnp.maximum(i - 1, 0)])
    gg_ref[...] = total[:, 0:TOK]

    for i in range(1, ND):
        to_dp(i).wait_send()
    for kind in range(3):
        for d in range(2):
            to_x(kind, d).wait_send()


def body(out_grad, expert_ids, gates, hidden_saved, w_down):
    any_spec = pl.BlockSpec(memory_space=pl.ANY)
    vmem = pl.BlockSpec(memory_space=pltpu.VMEM)
    half = FQ // 2
    dma = pltpu.SemaphoreType.DMA
    d_hidden, w_grad, gate_grad = pl.pallas_call(
        kernel,
        out_shape=(
            pltpu.VMEM((NZ, CAP, SH), BF),
            pltpu.VMEM((FQ, WID), F32),
            pltpu.VMEM((8, TOK), F32),
        ),
        in_specs=[any_spec] * 5,
        out_specs=[vmem, vmem, vmem],
        scratch_shapes=[
            pltpu.VMEM((NZ, ROWS, 128), BF),
            pltpu.VMEM((8, TOK), jnp.int32),
            pltpu.VMEM((8, TOK), BF),
            pltpu.VMEM((NZ, CAP, FF), BF),
            pltpu.VMEM((2, 4, SH, WID), BF),
            pltpu.VMEM((NC, FQ, WID), F32),
            pltpu.VMEM((GR, WID), BF),
            pltpu.VMEM((GR, WID), BF),
            pltpu.VMEM((4, GR, SH), BF),
            pltpu.VMEM((2, 128, 256), F32),
            pltpu.VMEM((GR, 1), F32),
            pltpu.VMEM((GR, SH), F32),
            pltpu.VMEM((NG, 4, GR, SH), BF),
            pltpu.VMEM((NG, 4, GR, SH), BF),
            pltpu.VMEM((NG, 3, GR, SH), BF),
            pltpu.VMEM((NG, 3, GR, SH), BF),
            pltpu.VMEM((NZ // 2, 1, 128), F32),
            pltpu.VMEM((NZ, 1, 128), F32),
            pltpu.VMEM((8, 128), F32),
            pltpu.VMEM((ND - 1, 8, 128), F32),
            pltpu.VMEM((2, half, WID), BF),
            pltpu.VMEM((2, half, WID), BF),
            pltpu.VMEM((2, half, WID), BF),
            pltpu.VMEM((2, half, WID), BF),
            pltpu.VMEM((2, half, WID), BF),
            pltpu.VMEM((2, half, WID), BF),
            dma((5 + TILES,)),
            dma((2, NCH, 16)),
            dma((2, NCH, 16)),
            dma((NG,)),
            dma((NG,)),
            dma((NG, 3)),
            dma((NG, 3)),
            dma((NZ,)),
            dma((NZ,)),
            dma((ND - 1,)),
            dma((ND - 1,)),
            dma((3, 2)),
            dma((3, 2)),
        ],
        compiler_params=pltpu.CompilerParams(
            collective_id=0, has_side_effects=True, vmem_limit_bytes=60 * 2**20
        ),
        cost_estimate=pl.CostEstimate(
            flops=4 * 1024 * 1024 * 896, bytes_accessed=6 * 2**20, transcendentals=0
        ),
    )(
        out_grad,
        expert_ids.T,
        gates.T,
        hidden_saved.reshape(NZ, CAP, FF),
        w_down.reshape(4, 2, SH, WID),
    )
    return (
        d_hidden.reshape(NZ * CAP, SH),
        w_grad.reshape(1, FQ, WID),
        gate_grad.T,
    )


def solution(mesh):
    return jax.shard_map(
        body,
        mesh=mesh,
        in_specs=(
            P(("ctx", "expert"), "dp"),
            P(("ctx", "expert"), None),
            P(("ctx", "expert"), None),
            P(("ctx", "expert"), None),
            P("expert", None, "dp"),
        ),
        out_specs=(
            P(("ctx", "expert"), "dp"),
            P("expert", "ctx", "dp"),
            P(("ctx", "expert"), None),
        ),
        check_vma=False,
    )
```
